32 devices in a mesh: group: 8 (over y, x, core), replica: 4 (over z).
Axes of the slice: x: 2, y: 2, z: 4, core: 2. Of those that a mesh axis runs over, the one named last changes fastest.
Arguments:
- tokens: bfloat16 [4, 1024, 960], P('replica', 'group'), may hold values from -6 to 6
- positions: int32 [4, 1024], P('replica', 'group'), may hold values from 0 to 999, as said below
- gain_attn: bfloat16 [2, 960], P(None, 'group'), may hold values from 0.5 to 1.5
- w_query: bfloat16 [2, 960, 960], P(None, 'group'), may hold values from -0.1875 to 0.1875
- w_key: bfloat16 [2, 960, 320], P(None, 'group'), may hold values from -0.1875 to 0.1875
- w_value: bfloat16 [2, 960, 320], P(None, 'group'), may hold values from -0.1875 to 0.1875
- w_out: bfloat16 [2, 960, 960], P(None, 'group'), may hold values from -0.5 to 0.5
- gain_ffn: bfloat16 [2, 960], P(None, 'group'), may hold values from 0.5 to 1.5
- w_gate: bfloat16 [2, 960, 2560], P(None, 'group'), may hold values from -0.1875 to 0.1875
- w_up: bfloat16 [2, 960, 2560], P(None, 'group'), may hold values from -0.1875 to 0.1875
- w_down: bfloat16 [2, 2560, 960], P(None, 'group'), may hold values from -0.125 to 0.125
- cotangent: bfloat16 [4, 1024, 960], P('replica', 'group'), may hold values from -6 to 6
Outputs:
- activations: float32 [4, 2, 1024, 960], P('replica', None, 'group')
- grad_tokens: float32 [4, 1024, 960], P('replica', 'group')
- grad_gain_attn: float32 [2, 960], P(None, 'group')
- grad_w_query: float32 [2, 960, 960], P(None, 'group')
- grad_w_key: float32 [2, 960, 320], P(None, 'group')
- grad_w_value: float32 [2, 960, 320], P(None, 'group')
- grad_w_out: float32 [2, 960, 960], P(None, 'group')
- grad_gain_ffn: float32 [2, 960], P(None, 'group')
- grad_w_gate: float32 [2, 960, 2560], P(None, 'group')
- grad_w_up: float32 [2, 960, 2560], P(None, 'group')
- grad_w_down: float32 [2, 2560, 960], P(None, 'group')
The draws below stay inside these ranges and needn't reach their ends.
Inputs may be any that keep to these rules, and one draw needn't show every extreme that they name: In each sequence positions are 0 at a document's first token and rise by one per token inside a document; every document except a sequence's last has 100 to 1000 tokens; the first token of every sequence has position 0.
All inputs are finite; a program needn't handle non-finite values.
Results may differ from the reference program's by a relative error of at most 0.02.
Values may be sent and summed in bfloat16 or wider, within the bound.
A program may use at most 320 MiB of HBM per device.

```python
import jax
import jax.numpy as jnp
from jax import lax

D = 960
HEADS = 15
KV_HEADS = 5
HEAD_DIM = 64
FF = 2560
LAYERS = 2
LEN = 1024
SEQS = 4
DOC_LEAST = 100
DOC_MOST = 1000


def draw_positions(key, part):
    doc_count = LEN // DOC_LEAST + 1
    doc_sizes = jax.random.randint(jax.random.fold_in(key, 11), (SEQS, doc_count), DOC_LEAST, DOC_MOST + 1)
    chosen_seq = jax.random.randint(jax.random.fold_in(key, 13), (), 0, SEQS)
    first_column = jnp.arange(doc_count, dtype=jnp.int32)[None, :] == 0
    chosen_rows = jnp.arange(SEQS, dtype=jnp.int32)[:, None] == chosen_seq
    doc_sizes = jnp.where(first_column & chosen_rows, DOC_MOST, doc_sizes).astype(jnp.int32)
    doc_starts = jnp.cumsum(doc_sizes, axis=1) - doc_sizes
    token_index = jnp.arange(LEN, dtype=jnp.int32)
    is_start = jnp.any(token_index[None, :, None] == doc_starts[:, None, :], axis=2)
    latest = lax.cummax(jnp.where(is_start, token_index[None, :], 0), axis=1)
    return (token_index[None, :] - latest).astype(jnp.int32)


def shard_levels(rng, dims, shards, least, largest):
    loudness, own = 1.0, jax.random.fold_in(rng, 6)
    for dim, parts in shards:
        heights = jnp.exp(jax.random.uniform(jax.random.fold_in(own, dim), (parts,), jnp.float32, least / len(shards), largest / len(shards)))
        loudness = loudness * jnp.repeat(heights, dims[dim] // parts).reshape([-1 if axis == dim else 1 for axis in range(len(dims))])
    return loudness


def centred(rng, shape, scale, most, split=(), kind=jnp.bfloat16):
    level = shard_levels(rng, shape, split, -0.22, 0.18) if split else 1.0
    array = jax.random.normal(rng, shape, jnp.float32) * scale * level
    return jnp.minimum(jnp.maximum(array, -most), most).astype(kind)


def setup_inputs(seed: int = 0) -> dict:
    streams_of = jax.random.split(jax.random.key(seed), 13)
    return {
        "tokens": centred(streams_of[0], (SEQS, LEN, D), 1.0, 6.0, ((0, 4), (1, 8))),
        "positions": draw_positions(jax.random.fold_in(streams_of[12], 71), 0),
        "gain_attn": jnp.clip(1.0 + 0.1 * jax.random.normal(streams_of[2], (LAYERS, D), jnp.float32), 0.5, 1.5).astype(jnp.bfloat16),
        "w_query": centred(streams_of[3], (LAYERS, D, HEADS * HEAD_DIM), D ** -0.5, 0.1875, ((1, 8),)),
        "w_key": centred(streams_of[4], (LAYERS, D, KV_HEADS * HEAD_DIM), D ** -0.5, 0.1875, ((1, 8),)),
        "w_value": centred(streams_of[5], (LAYERS, D, KV_HEADS * HEAD_DIM), D ** -0.5, 0.1875, ((1, 8),)),
        "w_out": centred(streams_of[6], (LAYERS, HEADS * HEAD_DIM, D), (HEADS * HEAD_DIM // 8) ** -0.5, 0.5, ((1, 8),)),
        "gain_ffn": jnp.clip(1.0 + 0.1 * jax.random.normal(streams_of[7], (LAYERS, D), jnp.float32), 0.5, 1.5).astype(jnp.bfloat16),
        "w_gate": centred(streams_of[8], (LAYERS, D, FF), D ** -0.5, 0.1875, ((1, 8),)),
        "w_up": centred(streams_of[9], (LAYERS, D, FF), D ** -0.5, 0.1875, ((1, 8),)),
        "w_down": centred(streams_of[10], (LAYERS, FF, D), FF ** -0.5, 0.125, ((1, 8),)),
        "cotangent": centred(streams_of[11], (SEQS, LEN, D), 1.0, 6.0, ((0, 4), (1, 8))),
    }


@jax.custom_vjp
def low(v):
    return lax.optimization_barrier(v.astype(jnp.bfloat16)).astype(jnp.float32)

@jax.custom_vjp
def low_back(v):
    return v

def low_keep(v):
    return (low(v), None)

def low_pass(kept, grad):
    return (grad,)

def back_keep(v):
    return (v, None)

def back_low(kept, grad):
    return (low(grad),)
low.defvjp(low_keep, low_pass)
low_back.defvjp(back_keep, back_low)
epsilon = 1e-05
rope_base = 100000.0
highest = lax.Precision.HIGHEST

def product(left, right):
    return jnp.dot(left, right, precision=highest, preferred_element_type=jnp.float32)

def rope_tables(token_positions):
    half_dim = HEAD_DIM // 2
    frequency = rope_base ** (-2.0 * jnp.arange(half_dim, dtype=jnp.float32) / HEAD_DIM)
    angles = token_positions.astype(jnp.float32)[:, None] * frequency[None, :]
    return (jnp.cos(angles)[:, None, :], jnp.sin(angles)[:, None, :])

def rotate(vectors, cosine, sine_table):
    half_dim = HEAD_DIM // 2
    leading, trailing = (vectors[..., :half_dim], vectors[..., half_dim:])
    return jnp.concatenate([leading * cosine - trailing * sine_table, trailing * cosine + leading * sine_table], axis=-1)

def rms_norm(stream, gain):
    return stream * lax.rsqrt(lax.optimization_barrier(jnp.mean(stream * stream, axis=-1, keepdims=True)) + epsilon) * gain

def attend(queries, keys_all, values_all, token_positions):
    block = min(512, LEN)
    block_count = LEN // block
    groups = HEADS // KV_HEADS
    blocked = queries.reshape(block_count, block, KV_HEADS, groups, HEAD_DIM)
    row_index = jnp.arange(LEN, dtype=jnp.int32)
    firsts = (row_index - token_positions.astype(jnp.int32)).reshape(block_count, block)
    rows_blocked = row_index.reshape(block_count, block)

    def one_block(pieces):
        block_queries, block_first, block_rows = pieces
        scores = jnp.einsum('qkgd,skd->kgqs', block_queries, keys_all, precision=highest) * 0.125
        scores = low_back(scores)
        allowed = (row_index[None, :] <= block_rows[:, None]) & (row_index[None, :] >= block_first[:, None])
        scores = jnp.where(allowed, scores, -1e+30)
        row_max = lax.optimization_barrier(jnp.max(scores, axis=-1, keepdims=True))
        exponent = jnp.exp(scores - row_max)
        weights_soft = low(exponent / lax.optimization_barrier(jnp.sum(exponent, axis=-1, keepdims=True)))
        return jnp.einsum('kgqs,skd->qkgd', weights_soft, values_all, precision=highest)
    mixed_heads = lax.map(jax.checkpoint(one_block), (blocked, firsts, rows_blocked))
    return mixed_heads.reshape(LEN, HEADS * HEAD_DIM)

def layer(stream, token_positions, params):
    gain_attn, w_query, w_key, w_value, w_out, gain_ffn, w_gate, w_up, w_down = params
    cosine, sine_table = rope_tables(token_positions)
    normed = low(rms_norm(stream, gain_attn))
    queries = low_back(product(normed, w_query)).reshape(LEN, HEADS, HEAD_DIM)
    queries = low(rotate(queries, cosine, sine_table))
    keys_all = low_back(product(normed, w_key)).reshape(LEN, KV_HEADS, HEAD_DIM)
    keys_all = low(rotate(keys_all, cosine, sine_table))
    values_all = low(low_back(product(normed, w_value))).reshape(LEN, KV_HEADS, HEAD_DIM)
    mixed_heads = low(low_back(attend(queries, keys_all, values_all, token_positions)))
    after_attn = stream + low_back(product(mixed_heads, w_out))
    normed_ffn = low(rms_norm(after_attn, gain_ffn))
    gate_value = low_back(product(normed_ffn, w_gate))
    up_value = low_back(product(normed_ffn, w_up))
    hidden = low(jax.nn.silu(gate_value) * up_value)
    return after_attn + low_back(product(hidden, w_down))

def reference(tokens, positions, gain_attn, w_query, w_key, w_value, w_out, gain_ffn, w_gate, w_up, w_down, cotangent):
    weights = tuple((w.astype(jnp.float32) for w in (gain_attn, w_query, w_key, w_value, w_out, gain_ffn, w_gate, w_up, w_down)))

    def forward(stream_all, params):

        def one_sequence(pieces):
            stream, token_positions = pieces
            outputs = []
            for layer_index in range(LAYERS):
                stream = layer(stream, token_positions, tuple((p[layer_index] for p in params)))
                outputs.append(stream)
            return jnp.stack(outputs)
        return lax.map(one_sequence, (stream_all, positions))
    activations, pullback = jax.vjp(forward, tokens.astype(jnp.float32), weights)
    start_grad = jnp.zeros_like(activations).at[:, LAYERS - 1].set(cotangent.astype(jnp.float32))
    grad_tokens, grads = pullback(start_grad)
    return (activations, grad_tokens, grads[0], grads[1], grads[2], grads[3], grads[4], grads[5], grads[6], grads[7], grads[8])
```

```python
import jax
import jax.numpy as jnp
from jax import lax
from jax.experimental import pallas as pl
from jax.experimental.pallas import tpu as pltpu
from jax.sharding import PartitionSpec as P

HEADS = 15
KV_HEADS = 5
HEAD_DIM = 64
LAYERS = 2
SHARE = HEADS // KV_HEADS

epsilon = 1e-05
rope_base = 100000.0
low = jnp.bfloat16


def dot(left, right):
    return jnp.dot(left, right, preferred_element_type=jnp.float32)


def over_rows(left, right):
    return lax.dot_general(
        left, right, (((0,), (0,)), ((), ())), preferred_element_type=jnp.float32
    )


def against(left, right):
    return lax.dot_general(
        left, right, (((1,), (1,)), ((), ())), preferred_element_type=jnp.float32
    )


def gather_kernel(members, block_ref, out_ref, local_sem, send_sem, recv_sem, pass_sem, got_sem):
    me = lax.axis_index("group")
    chips = members // 2
    chip, core = lax.div(me, 2), lax.rem(me, 2)
    sibling = chip * 2 + 1 - core
    barrier = pltpu.get_barrier_semaphore()
    pl.semaphore_signal(barrier, inc=1, device_id={"group": sibling})
    for step in range(1, chips):
        peer = lax.rem(chip + step, chips) * 2 + core
        pl.semaphore_signal(barrier, inc=1, device_id={"group": peer})
    pl.semaphore_wait(barrier, chips)
    sends = []
    for step in range(1, chips):
        peer = lax.rem(chip + step, chips) * 2 + core
        copy = pltpu.make_async_remote_copy(
            src_ref=block_ref,
            dst_ref=out_ref.at[me],
            send_sem=send_sem.at[step],
            recv_sem=recv_sem.at[step],
            device_id={"group": peer},
        )
        copy.start()
        sends.append(copy)
    own = pltpu.make_async_remote_copy(
        src_ref=block_ref,
        dst_ref=out_ref.at[me],
        send_sem=pass_sem.at[0],
        recv_sem=got_sem.at[0],
        device_id={"group": sibling},
    )
    own.start()
    local = pltpu.make_async_copy(block_ref, out_ref.at[me], local_sem)
    local.start()
    passes = [own]
    for step in range(1, chips):
        sends[step - 1].wait_recv()
        source = lax.rem(chip - step + chips, chips) * 2 + core
        copy = pltpu.make_async_remote_copy(
            src_ref=out_ref.at[source],
            dst_ref=out_ref.at[source],
            send_sem=pass_sem.at[step],
            recv_sem=got_sem.at[step],
            device_id={"group": sibling},
        )
        copy.start()
        passes.append(copy)
    local.wait()
    for copy in passes:
        copy.wait()
    for copy in sends:
        copy.wait_send()


def gather(block, members):
    rows, width = block.shape
    out = pl.pallas_call(
        lambda *refs: gather_kernel(members, *refs),
        out_shape=jax.ShapeDtypeStruct((members, rows, width), block.dtype),
        in_specs=[pl.BlockSpec(memory_space=pltpu.VMEM)],
        out_specs=pl.BlockSpec(memory_space=pltpu.VMEM),
        scratch_shapes=[pltpu.SemaphoreType.DMA]
        + [pltpu.SemaphoreType.DMA((members // 2,)) for _ in range(4)],
        compiler_params=pltpu.CompilerParams(
            collective_id=0, has_side_effects=True, vmem_limit_bytes=24 * 2**20
        ),
        cost_estimate=pl.CostEstimate(
            flops=0, bytes_accessed=30_000_000, transcendentals=0
        ),
    )(block)
    return out.reshape(members * rows, width)


def scatter_kernel(
    members, part_ref, out_ref, pair_ref, ready_ref, land_ref, pair_send, pair_recv, send_sem, recv_sem
):
    me = lax.axis_index("group")
    chips = members // 2
    chip, core = lax.div(me, 2), lax.rem(me, 2)
    sibling = chip * 2 + 1 - core
    barrier = pltpu.get_barrier_semaphore()
    pl.semaphore_signal(barrier, inc=1, device_id={"group": sibling})
    for step in range(1, chips):
        peer = lax.rem(chip + step, chips) * 2 + core
        pl.semaphore_signal(barrier, inc=1, device_id={"group": peer})
    pl.semaphore_wait(barrier, chips)
    pairs = []
    for step in range(chips):
        place = lax.rem(chip + step + 1, chips)
        copy = pltpu.make_async_remote_copy(
            src_ref=part_ref.at[place * 2 + 1 - core],
            dst_ref=pair_ref.at[step],
            send_sem=pair_send.at[step],
            recv_sem=pair_recv.at[step],
            device_id={"group": sibling},
        )
        copy.start()
        pairs.append(copy)
    sends = []
    for step in range(chips):
        place = lax.rem(chip + step + 1, chips)
        pairs[step].wait_recv()
        total = part_ref[place * 2 + core].astype(jnp.float32) + pair_ref[step].astype(jnp.float32)
        if step == chips - 1:
            out_ref[...] = total
            break
        ready_ref[step] = total.astype(low)
        copy = pltpu.make_async_remote_copy(
            src_ref=ready_ref.at[step],
            dst_ref=land_ref.at[step],
            send_sem=send_sem.at[step],
            recv_sem=recv_sem.at[step],
            device_id={"group": place * 2 + core},
        )
        copy.start()
        sends.append(copy)
    for step in range(chips - 1):
        sends[step].wait_recv()
        out_ref[...] += land_ref[step].astype(jnp.float32)
    for copy in pairs + sends:
        copy.wait_send()


def scatter_sum(partial, members):
    length, width = partial.shape
    rows = length // members
    chips = members // 2
    return pl.pallas_call(
        lambda *refs: scatter_kernel(members, *refs),
        out_shape=jax.ShapeDtypeStruct((rows, width), jnp.float32),
        in_specs=[pl.BlockSpec(memory_space=pltpu.VMEM)],
        out_specs=pl.BlockSpec(memory_space=pltpu.VMEM),
        scratch_shapes=[
            pltpu.VMEM((chips, rows, width), low),
            pltpu.VMEM((chips, rows, width), low),
            pltpu.VMEM((chips, rows, width), low),
        ]
        + [pltpu.SemaphoreType.DMA((chips,)) for _ in range(4)],
        compiler_params=pltpu.CompilerParams(
            collective_id=1, has_side_effects=True, vmem_limit_bytes=24 * 2**20
        ),
        cost_estimate=pl.CostEstimate(
            flops=0, bytes_accessed=30_000_000, transcendentals=0
        ),
    )(partial.astype(low).reshape(members, rows, width))


def swap(blocks):
    return lax.all_to_all(blocks, "group", split_axis=0, concat_axis=0, tiled=True)


def rope_tables(token_positions):
    half_dim = HEAD_DIM // 2
    frequency = rope_base ** (-2.0 * jnp.arange(half_dim, dtype=jnp.float32) / HEAD_DIM)
    angles = token_positions.astype(jnp.float32)[:, None] * frequency[None, :]
    return (jnp.cos(angles)[:, None, :], jnp.sin(angles)[:, None, :])


def rotate(vectors, cosine, sine_table):
    half_dim = HEAD_DIM // 2
    leading, trailing = (vectors[..., :half_dim], vectors[..., half_dim:])
    return jnp.concatenate(
        [leading * cosine - trailing * sine_table, trailing * cosine + leading * sine_table],
        axis=-1,
    )


def norm_forward(stream):
    inverse = lax.rsqrt(jnp.mean(stream * stream, axis=-1, keepdims=True) + epsilon)
    return (inverse, stream * inverse)


def norm_back(grad_unit, unit_value, inverse):
    return inverse * (
        grad_unit - unit_value * jnp.mean(grad_unit * unit_value, axis=-1, keepdims=True)
    )


def pad_columns(matrix, width):
    return jnp.pad(matrix, ((0, 0), (0, width - matrix.shape[1])))


def widen(matrix):
    rows = matrix.shape[0]
    wide = matrix.reshape(rows, KV_HEADS, 1, HEAD_DIM)
    wide = jnp.broadcast_to(wide, (rows, KV_HEADS, SHARE, HEAD_DIM))
    return wide.reshape(rows, HEADS * HEAD_DIM)


def by_member(matrix, members):
    rows, width = matrix.shape
    return matrix.reshape(rows, members, width // members).transpose(1, 0, 2)


def by_row(blocks):
    members, rows, width = blocks.shape
    return blocks.transpose(1, 0, 2).reshape(rows, members * width)


def on_device(
    tokens,
    positions,
    gain_attn,
    w_query,
    w_key,
    w_value,
    w_out,
    gain_ffn,
    w_gate,
    w_up,
    w_down,
    cotangent,
):
    row_count = tokens.shape[1]
    members = lax.axis_size("group")
    owner = lax.axis_index("group")
    length = row_count * members
    own_rows = w_query.shape[1]
    width = own_rows * members
    local_heads = -(-HEADS // members)
    span = local_heads * HEAD_DIM
    padded = span * members
    part_ff = w_gate.shape[2] // members

    all_positions = lax.all_gather(positions[0], "group", axis=0, tiled=True)
    gains = lax.all_gather(
        jnp.concatenate([gain_attn, gain_ffn], axis=0), "group", axis=1, tiled=True
    ).astype(jnp.float32)

    weights = []
    for layer in range(LAYERS):
        attn_blocks = jnp.concatenate(
            [
                by_member(pad_columns(w_query[layer], padded), members),
                by_member(pad_columns(widen(w_key[layer]), padded), members),
                by_member(pad_columns(widen(w_value[layer]), padded), members),
            ],
            axis=2,
        )
        ffn_blocks = jnp.concatenate(
            [by_member(w_gate[layer], members), by_member(w_up[layer], members)], axis=2
        )
        attn_weight = swap(attn_blocks).reshape(width, 3 * span)
        ffn_weight = swap(ffn_blocks).reshape(width, 2 * part_ff)
        weights.append([attn_weight, ffn_weight])
    next_out = lax.ppermute(
        w_out, "group", [(member, member - 1) for member in range(1, members)]
    )
    slab = jnp.concatenate(
        [w_out, next_out, jnp.zeros((LAYERS, span - own_rows, width), w_out.dtype)], axis=1
    )
    out_all = lax.dynamic_slice_in_dim(slab, owner * (span - own_rows), span, 1)

    token_index = jnp.arange(length, dtype=jnp.int32)
    allowed = (token_index[None, :] <= token_index[:, None]) & (
        token_index[None, :] >= (token_index - all_positions)[:, None]
    )
    cosine, sine_table = rope_tables(all_positions)

    def heads_of(matrix):
        return matrix.reshape(length, local_heads, HEAD_DIM)

    stream = tokens[0].astype(jnp.float32)
    saved_all = []
    outputs = []
    for layer in range(LAYERS):
        attn_weight, ffn_weight = weights[layer]
        inverse_attn, unit_attn = norm_forward(stream)
        normed_attn = gather((unit_attn * gains[layer]).astype(low), members)
        product = dot(normed_attn, attn_weight)
        queries = rotate(heads_of(product[:, :span]), cosine, sine_table).astype(low)
        keys = rotate(heads_of(product[:, span : 2 * span]), cosine, sine_table).astype(low)
        values = heads_of(product[:, 2 * span :]).astype(low)
        scores = (
            jnp.einsum("thd,shd->hts", queries, keys, preferred_element_type=jnp.float32) * 0.125
        )
        scores = jnp.where(allowed[None], scores, -1e30)
        exponent = jnp.exp(scores - jnp.max(scores, axis=-1, keepdims=True))
        probs = (exponent / jnp.sum(exponent, axis=-1, keepdims=True)).astype(low)
        mixed = jnp.einsum("hts,shd->thd", probs, values, preferred_element_type=jnp.float32)
        mixed = mixed.reshape(length, span).astype(low)
        after = stream + scatter_sum(dot(mixed, out_all[layer]), members)
        inverse_ffn, unit_ffn = norm_forward(after)
        normed_ffn = gather((unit_ffn * gains[LAYERS + layer]).astype(low), members)
        both = dot(normed_ffn, ffn_weight)
        gate, up = both[:, :part_ff], both[:, part_ff:]
        hidden = (jax.nn.silu(gate) * up).astype(low)
        stream = after + scatter_sum(dot(hidden, w_down[layer]), members)
        outputs.append(stream)
        saved_all.append(
            (
                inverse_attn, unit_attn, normed_attn, queries, keys, values, probs, mixed,
                inverse_ffn, unit_ffn, normed_ffn, gate, up, hidden,
            )
        )

    grad_result = cotangent[0].astype(jnp.float32)
    owned = [None] * LAYERS
    gain_sums = [None] * (2 * LAYERS)
    for layer in reversed(range(LAYERS)):
        attn_weight, ffn_weight = weights[layer]
        (
            inverse_attn, unit_attn, normed_attn, queries, keys, values, probs, mixed,
            inverse_ffn, unit_ffn, normed_ffn, gate, up, hidden,
        ) = saved_all[layer]
        out_low = gather(grad_result.astype(low), members)
        grad_hidden = against(out_low, w_down[layer])
        sigmoid = jax.nn.sigmoid(gate)
        grad_up = (grad_hidden * gate * sigmoid).astype(low)
        grad_gate = (grad_hidden * up * sigmoid * (1.0 + gate * (1.0 - sigmoid))).astype(low)
        grad_both = jnp.concatenate([grad_gate, grad_up], axis=1)
        grad_normed_ffn = scatter_sum(against(grad_both, ffn_weight), members)
        grad_down = over_rows(hidden, out_low).astype(low)
        grad_ffn_weight = swap(
            over_rows(normed_ffn, grad_both).astype(low).reshape(members, own_rows, 2 * part_ff)
        )
        gain_sums[LAYERS + layer] = jnp.sum(grad_normed_ffn * unit_ffn, axis=0)
        grad_after = grad_result + norm_back(
            grad_normed_ffn * gains[LAYERS + layer], unit_ffn, inverse_ffn
        )
        after_low = gather(grad_after.astype(low), members)
        grad_mixed = against(after_low, out_all[layer]).astype(low)
        grad_out = over_rows(mixed, after_low).astype(low)
        delta = jnp.sum(
            heads_of(grad_mixed.astype(jnp.float32) * mixed.astype(jnp.float32)), axis=-1
        ).T[:, :, None]
        grad_heads = heads_of(grad_mixed)
        grad_probs = jnp.einsum(
            "thd,shd->hts", grad_heads, values, preferred_element_type=jnp.float32
        )
        grad_values = jnp.einsum(
            "hts,thd->shd", probs, grad_heads, preferred_element_type=jnp.float32
        )
        grad_scores = (probs.astype(jnp.float32) * (grad_probs - delta)).astype(low)
        grad_queries = 0.125 * jnp.einsum(
            "hts,shd->thd", grad_scores, keys, preferred_element_type=jnp.float32
        )
        grad_keys = 0.125 * jnp.einsum(
            "hts,thd->shd", grad_scores, queries, preferred_element_type=jnp.float32
        )
        back = jnp.concatenate(
            [
                rotate(grad_queries, cosine, -sine_table).reshape(length, span),
                rotate(grad_keys, cosine, -sine_table).reshape(length, span),
                grad_values.reshape(length, span),
            ],
            axis=1,
        ).astype(low)
        grad_normed_attn = scatter_sum(against(back, attn_weight), members)
        grad_attn_weight = swap(
            over_rows(normed_attn, back).astype(low).reshape(members, own_rows, 3 * span)
        )
        gain_sums[layer] = jnp.sum(grad_normed_attn * unit_attn, axis=0)
        grad_result = grad_after + norm_back(
            grad_normed_attn * gains[layer], unit_attn, inverse_attn
        )

        before = lax.ppermute(
            grad_out, "group", [(member, member + 1) for member in range(members - 1)]
        )
        own_out = lax.dynamic_slice_in_dim(
            jnp.concatenate([before, grad_out], axis=0),
            span - owner * (span - own_rows),
            own_rows,
            0,
        )

        def narrow(blocks):
            wide = by_row(blocks)[:, : HEADS * HEAD_DIM].astype(jnp.float32)
            wide = wide.reshape(own_rows, KV_HEADS, SHARE, HEAD_DIM)
            return wide.sum(axis=2).reshape(own_rows, KV_HEADS * HEAD_DIM).astype(low)

        shares = (
            by_row(grad_attn_weight[:, :, :span])[:, : HEADS * HEAD_DIM],
            narrow(grad_attn_weight[:, :, span : 2 * span]),
            narrow(grad_attn_weight[:, :, 2 * span :]),
            own_out,
            by_row(grad_ffn_weight[:, :, :part_ff]),
            by_row(grad_ffn_weight[:, :, part_ff:]),
            grad_down,
        )
        if layer + 1 < LAYERS:
            shares, owned[layer + 1] = lax.optimization_barrier((shares, owned[layer + 1]))
        owned[layer] = lax.psum(shares, "replica")

    gain_total = lax.psum(jnp.stack(gain_sums), ("group", "replica"))
    gain_total = lax.dynamic_slice_in_dim(gain_total, owner * own_rows, own_rows, 1)
    stacked = [
        jnp.stack([owned[layer][place] for layer in range(LAYERS)]).astype(jnp.float32)
        for place in range(7)
    ]
    return (
        jnp.stack(outputs)[None],
        grad_result[None],
        gain_total[:LAYERS],
        stacked[0],
        stacked[1],
        stacked[2],
        stacked[3],
        gain_total[LAYERS:],
        stacked[4],
        stacked[5],
        stacked[6],
    )


def solution(mesh):
    rows = P(None, "group", None)
    in_specs = (
        P("replica", "group", None),
        P("replica", "group"),
        P(None, "group"),
        rows,
        rows,
        rows,
        rows,
        P(None, "group"),
        rows,
        rows,
        rows,
        P("replica", "group", None),
    )
    out_specs = (
        P("replica", None, "group", None),
        P("replica", "group", None),
        P(None, "group"),
        rows,
        rows,
        rows,
        rows,
        P(None, "group"),
        rows,
        rows,
        rows,
    )
    return jax.shard_map(
        on_device, mesh=mesh, in_specs=in_specs, out_specs=out_specs, check_vma=False
    )
```

```python
import jax
import jax.numpy as jnp
from jax import lax
from jax.experimental import pallas as pl
from jax.experimental.pallas import tpu as pltpu
from jax.sharding import PartitionSpec as P

HEADS = 15
KV_HEADS = 5
HEAD_DIM = 64
LAYERS = 2
SHARE = HEADS // KV_HEADS

epsilon = 1e-05
rope_base = 100000.0
low = jnp.bfloat16


def dot(left, right):
    return jnp.dot(left, right, preferred_element_type=jnp.float32)


def over_rows(left, right):
    return lax.dot_general(
        left, right, (((0,), (0,)), ((), ())), preferred_element_type=jnp.float32
    )


def against(left, right):
    return lax.dot_general(
        left, right, (((1,), (1,)), ((), ())), preferred_element_type=jnp.float32
    )


def greet(chips, chip, core, sibling):
    barrier = pltpu.get_barrier_semaphore()
    pl.semaphore_signal(barrier, inc=1, device_id={"group": sibling})
    for step in range(1, chips):
        peer = lax.rem(chip + step, chips) * 2 + core
        pl.semaphore_signal(barrier, inc=1, device_id={"group": peer})
    return barrier


def spread(chips, me, block_ref, out_ref, local_sem, send_sem, recv_sem, pass_sem, got_sem):
    chip, core = lax.div(me, 2), lax.rem(me, 2)
    sibling = chip * 2 + 1 - core
    sends = []
    for step in range(1, chips):
        peer = lax.rem(chip + step, chips) * 2 + core
        copy = pltpu.make_async_remote_copy(
            src_ref=block_ref,
            dst_ref=out_ref.at[me],
            send_sem=send_sem.at[step],
            recv_sem=recv_sem.at[step],
            device_id={"group": peer},
        )
        copy.start()
        sends.append(copy)
    own = pltpu.make_async_remote_copy(
        src_ref=block_ref,
        dst_ref=out_ref.at[me],
        send_sem=pass_sem.at[0],
        recv_sem=got_sem.at[0],
        device_id={"group": sibling},
    )
    own.start()
    local = pltpu.make_async_copy(block_ref, out_ref.at[me], local_sem)
    local.start()
    passes = [own]
    for step in range(1, chips):
        sends[step - 1].wait_recv()
        source = lax.rem(chip - step + chips, chips) * 2 + core
        copy = pltpu.make_async_remote_copy(
            src_ref=out_ref.at[source],
            dst_ref=out_ref.at[source],
            send_sem=pass_sem.at[step],
            recv_sem=got_sem.at[step],
            device_id={"group": sibling},
        )
        copy.start()
        passes.append(copy)
    local.wait()
    for copy in passes:
        copy.wait()
    for copy in sends:
        copy.wait_send()


def first_kernel(
    members, block_ref, small_ref, weight_ref, out_ref, few_ref, swapped_ref,
    local_sem, send_sem, recv_sem, pass_sem, got_sem, few_sem, few_recv, swap_sem, swap_recv, own_sem,
):
    me = lax.axis_index("group")
    chips = members // 2
    barrier = pltpu.get_barrier_semaphore()
    for step in range(1, members):
        peer = lax.rem(me + step, members)
        pl.semaphore_signal(barrier, inc=1, device_id={"group": peer})
    pl.semaphore_wait(barrier, members - 1)
    copies = []
    for step in range(1, members):
        peer = lax.rem(me + step, members)
        few = pltpu.make_async_remote_copy(
            src_ref=small_ref,
            dst_ref=few_ref.at[me],
            send_sem=few_sem.at[step],
            recv_sem=few_recv.at[step],
            device_id={"group": peer},
        )
        few.start()
        block = pltpu.make_async_remote_copy(
            src_ref=weight_ref.at[peer],
            dst_ref=swapped_ref.at[me],
            send_sem=swap_sem.at[step],
            recv_sem=swap_recv.at[step],
            device_id={"group": peer},
        )
        block.start()
        copies += [few, block]
    own_few = pltpu.make_async_copy(small_ref, few_ref.at[me], own_sem.at[0])
    own_few.start()
    own_block = pltpu.make_async_copy(weight_ref.at[me], swapped_ref.at[me], own_sem.at[1])
    own_block.start()
    spread(chips, me, block_ref, out_ref, local_sem, send_sem, recv_sem, pass_sem, got_sem)
    own_few.wait()
    own_block.wait()
    for copy in copies:
        copy.wait()


def vmem():
    return pl.BlockSpec(memory_space=pltpu.VMEM)


def first_exchange(block, small, weight, members):
    sems = pltpu.SemaphoreType.DMA((members,))
    return pl.pallas_call(
        lambda *refs: first_kernel(members, *refs),
        out_shape=[
            jax.ShapeDtypeStruct((members,) + block.shape, block.dtype),
            jax.ShapeDtypeStruct((members,) + small.shape, small.dtype),
            jax.ShapeDtypeStruct(weight.shape, weight.dtype),
        ],
        in_specs=[vmem()] * 3,
        out_specs=[vmem()] * 3,
        scratch_shapes=[pltpu.SemaphoreType.DMA] + [sems] * 8 + [pltpu.SemaphoreType.DMA((2,))],
        compiler_params=pltpu.CompilerParams(
            collective_id=0, has_side_effects=True, vmem_limit_bytes=24 * 2**20
        ),
        cost_estimate=pl.CostEstimate(flops=0, bytes_accessed=60_000_000, transcendentals=0),
    )(block, small, weight)


def sum_kernel(members, backward, gathers, *refs):
    refs = list(refs)
    left_ref, right_ref, stream_ref, gain_ref = refs[:4]
    refs = refs[4:]
    if backward:
        grad_ref = refs.pop(0)
    result_ref = refs.pop(0)
    if backward:
        gain_out_ref = refs.pop(0)
    if gathers:
        out_ref = refs.pop(0)
    give_ref, pair_ref, ready_ref, land_ref, total_ref, low_ref = refs[:6]
    pair_send, pair_recv, send_sem, recv_sem = refs[6:10]
    me = lax.axis_index("group")
    chips = members // 2
    chip, core = lax.div(me, 2), lax.rem(me, 2)
    sibling = chip * 2 + 1 - core
    barrier = greet(chips, chip, core, sibling)
    pairs = []
    for step in range(chips):
        place = lax.rem(chip + step + 1, chips)
        give_ref[step] = dot(left_ref[place * 2 + 1 - core], right_ref[...]).astype(low)
        if step == 0:
            pl.semaphore_wait(barrier, chips)
        copy = pltpu.make_async_remote_copy(
            src_ref=give_ref.at[step],
            dst_ref=pair_ref.at[step],
            send_sem=pair_send.at[step],
            recv_sem=pair_recv.at[step],
            device_id={"group": sibling},
        )
        copy.start()
        pairs.append(copy)
    sends = []
    for step in range(chips):
        place = lax.rem(chip + step + 1, chips)
        part = dot(left_ref[place * 2 + core], right_ref[...])
        pairs[step].wait_recv()
        part = part + pair_ref[step].astype(jnp.float32)
        if step == chips - 1:
            total_ref[...] = part
            break
        ready_ref[step] = part.astype(low)
        copy = pltpu.make_async_remote_copy(
            src_ref=ready_ref.at[step],
            dst_ref=land_ref.at[step],
            send_sem=send_sem.at[step],
            recv_sem=recv_sem.at[step],
            device_id={"group": place * 2 + core},
        )
        copy.start()
        sends.append(copy)
    for step in range(chips - 1):
        sends[step].wait_recv()
        total_ref[...] += land_ref[step].astype(jnp.float32)
    total = total_ref[...]
    if backward:
        inverse, unit = norm_forward(stream_ref[...])
        gain_out_ref[...] = jnp.sum(total * unit, axis=0, keepdims=True)
        result = grad_ref[...] + norm_back(total * gain_ref[...], unit, inverse)
        result_ref[...] = result
        low_ref[...] = result.astype(low)
    else:
        result = stream_ref[...] + total
        result_ref[...] = result
        if gathers:
            unit = norm_forward(result)[1]
            low_ref[...] = (unit * gain_ref[...]).astype(low)
    if gathers:
        spread(chips, me, low_ref, out_ref, *refs[10:])
    for copy in pairs + sends:
        copy.wait_send()


def block_sum(name, left, right, stream, gain, members, grad=None, gathers=True):
    rows, width = stream.shape
    chips = members // 2
    backward = grad is not None
    outs = [jax.ShapeDtypeStruct((rows, width), jnp.float32)]
    if backward:
        outs.append(jax.ShapeDtypeStruct((1, width), jnp.float32))
    if gathers:
        outs.append(jax.ShapeDtypeStruct((members, rows, width), low))
    operands = [left.reshape(members, rows, left.shape[1]), right, stream, gain[None]]
    if backward:
        operands.append(grad)
    sems = pltpu.SemaphoreType.DMA((chips,))
    scratch = [pltpu.VMEM((chips, rows, width), low) for _ in range(4)]
    scratch += [pltpu.VMEM((rows, width), jnp.float32), pltpu.VMEM((rows, width), low)]
    scratch += [sems] * 4
    if gathers:
        scratch += [pltpu.SemaphoreType.DMA] + [sems] * 4
    result = pl.pallas_call(
        lambda *refs: sum_kernel(members, backward, gathers, *refs),
        out_shape=outs,
        in_specs=[vmem()] * len(operands),
        out_specs=[vmem()] * len(outs),
        scratch_shapes=scratch,
        compiler_params=pltpu.CompilerParams(
            collective_id=name, has_side_effects=True, vmem_limit_bytes=32 * 2**20
        ),
        cost_estimate=pl.CostEstimate(flops=0, bytes_accessed=90_000_000, transcendentals=0),
    )(*operands)
    result = list(result)
    if gathers:
        result[-1] = result[-1].reshape(members * rows, width)
    return result


def swap(blocks):
    return lax.all_to_all(blocks, "group", split_axis=0, concat_axis=0, tiled=True)


def rope_tables(token_positions):
    half_dim = HEAD_DIM // 2
    frequency = rope_base ** (-2.0 * jnp.arange(half_dim, dtype=jnp.float32) / HEAD_DIM)
    angles = token_positions.astype(jnp.float32)[:, None] * frequency[None, :]
    return (jnp.cos(angles)[:, None, :], jnp.sin(angles)[:, None, :])


def rotate(vectors, cosine, sine_table):
    half_dim = HEAD_DIM // 2
    leading, trailing = (vectors[..., :half_dim], vectors[..., half_dim:])
    return jnp.concatenate(
        [leading * cosine - trailing * sine_table, trailing * cosine + leading * sine_table],
        axis=-1,
    )


def norm_forward(stream):
    inverse = lax.rsqrt(jnp.mean(stream * stream, axis=-1, keepdims=True) + epsilon)
    return (inverse, stream * inverse)


def norm_back(grad_unit, unit_value, inverse):
    return inverse * (
        grad_unit - unit_value * jnp.mean(grad_unit * unit_value, axis=-1, keepdims=True)
    )


def pad_columns(matrix, width):
    return jnp.pad(matrix, ((0, 0), (0, width - matrix.shape[1])))


def widen(matrix):
    rows = matrix.shape[0]
    wide = matrix.reshape(rows, KV_HEADS, 1, HEAD_DIM)
    wide = jnp.broadcast_to(wide, (rows, KV_HEADS, SHARE, HEAD_DIM))
    return wide.reshape(rows, HEADS * HEAD_DIM)


def by_member(matrix, members):
    rows, width = matrix.shape
    return matrix.reshape(rows, members, width // members).transpose(1, 0, 2)


def by_row(blocks):
    members, rows, width = blocks.shape
    return blocks.transpose(1, 0, 2).reshape(rows, members * width)


def on_device(
    tokens,
    positions,
    gain_attn,
    w_query,
    w_key,
    w_value,
    w_out,
    gain_ffn,
    w_gate,
    w_up,
    w_down,
    cotangent,
):
    row_count = tokens.shape[1]
    members = lax.axis_size("group")
    owner = lax.axis_index("group")
    length = row_count * members
    own_rows = w_query.shape[1]
    width = own_rows * members
    local_heads = -(-HEADS // members)
    span = local_heads * HEAD_DIM
    padded = span * members
    part_ff = w_gate.shape[2] // members

    def attn_blocks(layer):
        return jnp.concatenate(
            [
                by_member(pad_columns(w_query[layer], padded), members),
                by_member(pad_columns(widen(w_key[layer]), padded), members),
                by_member(pad_columns(widen(w_value[layer]), padded), members),
            ],
            axis=2,
        )

    def ffn_blocks(layer):
        return jnp.concatenate(
            [by_member(w_gate[layer], members), by_member(w_up[layer], members)], axis=2
        )

    lane = 128 * -(-max(row_count, own_rows) // 128)
    small = jnp.concatenate(
        [
            pad_columns(positions.astype(jnp.float32), lane),
            pad_columns(gain_attn.astype(jnp.float32), lane),
            pad_columns(gain_ffn.astype(jnp.float32), lane),
        ],
        axis=0,
    )
    small = jnp.pad(small, ((0, 8 - small.shape[0]), (0, 0)))
    token_blocks, few, first_weight = first_exchange(tokens[0], small, attn_blocks(0), members)
    all_positions = few[:, 0, :row_count].reshape(length).astype(jnp.int32)
    gains = few[:, 1 : 1 + 2 * LAYERS, :own_rows].transpose(1, 0, 2).reshape(2 * LAYERS, width)
    out_low = lax.all_gather(cotangent[0], "group", axis=0, tiled=True)

    weights = []
    for layer in range(LAYERS):
        attn_weight = first_weight if layer == 0 else swap(attn_blocks(layer))
        ffn_weight = swap(ffn_blocks(layer)).reshape(width, 2 * part_ff)
        weights.append([attn_weight.reshape(width, 3 * span), ffn_weight])
    next_out = lax.ppermute(
        w_out, "group", [(member, member - 1) for member in range(1, members)]
    )
    slab = jnp.concatenate(
        [w_out, next_out, jnp.zeros((LAYERS, span - own_rows, width), w_out.dtype)], axis=1
    )
    out_all = lax.dynamic_slice_in_dim(slab, owner * (span - own_rows), span, 1)

    token_index = jnp.arange(length, dtype=jnp.int32)
    allowed = (token_index[None, :] <= token_index[:, None]) & (
        token_index[None, :] >= (token_index - all_positions)[:, None]
    )
    cosine, sine_table = rope_tables(all_positions)

    def heads_of(matrix):
        return matrix.reshape(length, local_heads, HEAD_DIM)

    stream = tokens[0].astype(jnp.float32)
    unit_all = norm_forward(token_blocks.reshape(length, width).astype(jnp.float32))[1]
    normed_attn = (unit_all * gains[0]).astype(low)
    saved_all = []
    outputs = []
    for layer in range(LAYERS):
        attn_weight, ffn_weight = weights[layer]
        product = dot(normed_attn, attn_weight)
        queries = rotate(heads_of(product[:, :span]), cosine, sine_table).astype(low)
        keys = rotate(heads_of(product[:, span : 2 * span]), cosine, sine_table).astype(low)
        values = heads_of(product[:, 2 * span :]).astype(low)
        scores = (
            jnp.einsum("thd,shd->hts", queries, keys, preferred_element_type=jnp.float32) * 0.125
        )
        scores = jnp.where(allowed[None], scores, -1e30)
        exponent = jnp.exp(scores - jnp.max(scores, axis=-1, keepdims=True))
        probs = (exponent / jnp.sum(exponent, axis=-1, keepdims=True)).astype(low)
        mixed = jnp.einsum("hts,shd->thd", probs, values, preferred_element_type=jnp.float32)
        mixed = mixed.reshape(length, span).astype(low)
        after, normed_ffn = block_sum(
            1, mixed, out_all[layer], stream, gains[LAYERS + layer], members
        )
        both = dot(normed_ffn, ffn_weight)
        gate, up = both[:, :part_ff], both[:, part_ff:]
        hidden = (jax.nn.silu(gate) * up).astype(low)
        saved_all.append(
            (stream, normed_attn, queries, keys, values, probs, mixed, after, normed_ffn, gate, up, hidden)
        )
        if layer + 1 < LAYERS:
            stream, normed_attn = block_sum(
                2, hidden, w_down[layer], after, gains[layer + 1], members
            )
        else:
            stream = block_sum(
                3, hidden, w_down[layer], after, gains[layer], members, gathers=False
            )[0]
        outputs.append(stream)

    def narrow(blocks):
        wide = by_row(blocks)[:, : HEADS * HEAD_DIM].astype(jnp.float32)
        wide = wide.reshape(own_rows, KV_HEADS, SHARE, HEAD_DIM)
        return wide.sum(axis=2).reshape(own_rows, KV_HEADS * HEAD_DIM).astype(low)

    grad_result = cotangent[0].astype(jnp.float32)
    owned_attn = [None] * LAYERS
    owned_ffn = [None] * LAYERS
    gain_sums = [None] * (2 * LAYERS)
    previous = None

    def replica_sum(shares, previous):
        if previous is not None:
            shares, previous = lax.optimization_barrier((shares, previous))
        return lax.psum(shares, "replica"), previous

    for layer in reversed(range(LAYERS)):
        attn_weight, ffn_weight = weights[layer]
        (
            stream, normed_attn, queries, keys, values, probs, mixed, after, normed_ffn, gate, up, hidden
        ) = saved_all[layer]
        grad_hidden = against(out_low, w_down[layer])
        sigmoid = jax.nn.sigmoid(gate)
        grad_up = (grad_hidden * gate * sigmoid).astype(low)
        grad_gate = (grad_hidden * up * sigmoid * (1.0 + gate * (1.0 - sigmoid))).astype(low)
        grad_both = jnp.concatenate([grad_gate, grad_up], axis=1)
        grad_after, gain_sums[LAYERS + layer], after_low = block_sum(
            4, grad_both, ffn_weight.T, after, gains[LAYERS + layer], members, grad=grad_result
        )
        grad_down = over_rows(hidden, out_low).astype(low)
        grad_ffn_weight = swap(
            over_rows(normed_ffn, grad_both).astype(low).reshape(members, own_rows, 2 * part_ff)
        )
        after_low, grad_ffn_weight, grad_down = lax.optimization_barrier(
            (after_low, grad_ffn_weight, grad_down)
        )
        owned_ffn[layer], before = replica_sum(
            (
                by_row(grad_ffn_weight[:, :, :part_ff]),
                by_row(grad_ffn_weight[:, :, part_ff:]),
                grad_down,
            ),
            previous,
        )
        if before is not None:
            owned_attn[layer + 1] = before
        grad_mixed = against(after_low, out_all[layer]).astype(low)
        grad_out = over_rows(mixed, after_low).astype(low)
        delta = jnp.sum(
            heads_of(grad_mixed.astype(jnp.float32) * mixed.astype(jnp.float32)), axis=-1
        ).T[:, :, None]
        grad_heads = heads_of(grad_mixed)
        grad_probs = jnp.einsum(
            "thd,shd->hts", grad_heads, values, preferred_element_type=jnp.float32
        )
        grad_values = jnp.einsum(
            "hts,thd->shd", probs, grad_heads, preferred_element_type=jnp.float32
        )
        grad_scores = (probs.astype(jnp.float32) * (grad_probs - delta)).astype(low)
        grad_queries = 0.125 * jnp.einsum(
            "hts,shd->thd", grad_scores, keys, preferred_element_type=jnp.float32
        )
        grad_keys = 0.125 * jnp.einsum(
            "hts,thd->shd", grad_scores, queries, preferred_element_type=jnp.float32
        )
        back = jnp.concatenate(
            [
                rotate(grad_queries, cosine, -sine_table).reshape(length, span),
                rotate(grad_keys, cosine, -sine_table).reshape(length, span),
                grad_values.reshape(length, span),
            ],
            axis=1,
        ).astype(low)
        grad_attn_weight = swap(
            over_rows(normed_attn, back).astype(low).reshape(members, own_rows, 3 * span)
        )
        before = lax.ppermute(
            grad_out, "group", [(member, member + 1) for member in range(members - 1)]
        )
        own_out = lax.dynamic_slice_in_dim(
            jnp.concatenate([before, grad_out], axis=0),
            span - owner * (span - own_rows),
            own_rows,
            0,
        )
        if layer > 0:
            grad_result, gain_sums[layer], out_low = block_sum(
                5, back, attn_weight.T, stream, gains[layer], members, grad=grad_after
            )
            out_low, grad_attn_weight, own_out = lax.optimization_barrier(
                (out_low, grad_attn_weight, own_out)
            )
        else:
            grad_attn_weight, own_out, back = lax.optimization_barrier(
                (grad_attn_weight, own_out, back)
            )
            grad_result, gain_sums[layer] = block_sum(
                6, back, attn_weight.T, stream, gains[layer], members, grad=grad_after, gathers=False
            )
        previous, owned_ffn[layer] = replica_sum(
            (
                by_row(grad_attn_weight[:, :, :span])[:, : HEADS * HEAD_DIM],
                narrow(grad_attn_weight[:, :, span : 2 * span]),
                narrow(grad_attn_weight[:, :, 2 * span :]),
                own_out,
            ),
            owned_ffn[layer],
        )
    owned_attn[0] = previous

    gain_total = lax.psum(jnp.concatenate(gain_sums, axis=0), ("group", "replica"))
    gain_total = lax.dynamic_slice_in_dim(gain_total, owner * own_rows, own_rows, 1)
    stacked = [
        jnp.stack([(owned_attn[layer] + owned_ffn[layer])[place] for layer in range(LAYERS)]).astype(
            jnp.float32
        )
        for place in range(7)
    ]
    return (
        jnp.stack(outputs)[None],
        grad_result[None],
        gain_total[:LAYERS],
        stacked[0],
        stacked[1],
        stacked[2],
        stacked[3],
        gain_total[LAYERS:],
        stacked[4],
        stacked[5],
        stacked[6],
    )


def solution(mesh):
    rows = P(None, "group", None)
    in_specs = (
        P("replica", "group", None),
        P("replica", "group"),
        P(None, "group"),
        rows,
        rows,
        rows,
        rows,
        P(None, "group"),
        rows,
        rows,
        rows,
        P("replica", "group", None),
    )
    out_specs = (
        P("replica", None, "group", None),
        P("replica", "group", None),
        P(None, "group"),
        rows,
        rows,
        rows,
        rows,
        P(None, "group"),
        rows,
        rows,
        rows,
    )
    return jax.shard_map(
        on_device, mesh=mesh, in_specs=in_specs, out_specs=out_specs, check_vma=False
    )
```

```python
import jax
import jax.numpy as jnp
from jax import lax
from jax.experimental import pallas as pl
from jax.experimental.pallas import tpu as pltpu
from jax.sharding import PartitionSpec as P

HEADS = 15
KV_HEADS = 5
HEAD_DIM = 64
LAYERS = 2
SHARE = HEADS // KV_HEADS

epsilon = 1e-05
rope_base = 100000.0
low = jnp.bfloat16
COST = 3_000_000


def dot(left, right):
    return jnp.dot(left, right, preferred_element_type=jnp.float32)


def over_rows(left, right):
    return lax.dot_general(
        left, right, (((0,), (0,)), ((), ())), preferred_element_type=jnp.float32
    )


def against(left, right):
    return lax.dot_general(
        left, right, (((1,), (1,)), ((), ())), preferred_element_type=jnp.float32
    )


def greet(chips, chip, core, sibling):
    barrier = pltpu.get_barrier_semaphore()
    pl.semaphore_signal(barrier, inc=1, device_id={"group": sibling})
    for step in range(1, chips):
        peer = lax.rem(chip + step, chips) * 2 + core
        pl.semaphore_signal(barrier, inc=1, device_id={"group": peer})
    return barrier


def spread(chips, me, block_ref, out_ref, local_sem, send_sem, recv_sem, pass_sem, got_sem):
    chip, core = lax.div(me, 2), lax.rem(me, 2)
    sibling = chip * 2 + 1 - core
    sends = []
    for step in range(1, chips):
        peer = lax.rem(chip + step, chips) * 2 + core
        copy = pltpu.make_async_remote_copy(
            src_ref=block_ref,
            dst_ref=out_ref.at[me],
            send_sem=send_sem.at[step],
            recv_sem=recv_sem.at[step],
            device_id={"group": peer},
        )
        copy.start()
        sends.append(copy)
    own = pltpu.make_async_remote_copy(
        src_ref=block_ref,
        dst_ref=out_ref.at[me],
        send_sem=pass_sem.at[0],
        recv_sem=got_sem.at[0],
        device_id={"group": sibling},
    )
    own.start()
    local = pltpu.make_async_copy(block_ref, out_ref.at[me], local_sem)
    local.start()
    passes = [own]
    for step in range(1, chips):
        sends[step - 1].wait_recv()
        source = lax.rem(chip - step + chips, chips) * 2 + core
        copy = pltpu.make_async_remote_copy(
            src_ref=out_ref.at[source],
            dst_ref=out_ref.at[source],
            send_sem=pass_sem.at[step],
            recv_sem=got_sem.at[step],
            device_id={"group": sibling},
        )
        copy.start()
        passes.append(copy)
    local.wait()
    for copy in passes:
        copy.wait()
    for copy in sends:
        copy.wait_send()


def first_kernel(
    members, block_ref, small_ref, weight_ref, out_ref, few_ref, swapped_ref,
    local_sem, send_sem, recv_sem, pass_sem, got_sem, few_sem, few_recv, swap_sem, swap_recv, own_sem,
):
    me = lax.axis_index("group")
    chips = members // 2
    barrier = pltpu.get_barrier_semaphore()
    for step in range(1, members):
        peer = lax.rem(me + step, members)
        pl.semaphore_signal(barrier, inc=1, device_id={"group": peer})
    pl.semaphore_wait(barrier, members - 1)
    copies = []
    for step in range(1, members):
        peer = lax.rem(me + step, members)
        few = pltpu.make_async_remote_copy(
            src_ref=small_ref,
            dst_ref=few_ref.at[me],
            send_sem=few_sem.at[step],
            recv_sem=few_recv.at[step],
            device_id={"group": peer},
        )
        few.start()
        block = pltpu.make_async_remote_copy(
            src_ref=weight_ref.at[peer],
            dst_ref=swapped_ref.at[me],
            send_sem=swap_sem.at[step],
            recv_sem=swap_recv.at[step],
            device_id={"group": peer},
        )
        block.start()
        copies += [few, block]
    own_few = pltpu.make_async_copy(small_ref, few_ref.at[me], own_sem.at[0])
    own_few.start()
    own_block = pltpu.make_async_copy(weight_ref.at[me], swapped_ref.at[me], own_sem.at[1])
    own_block.start()
    spread(chips, me, block_ref, out_ref, local_sem, send_sem, recv_sem, pass_sem, got_sem)
    own_few.wait()
    own_block.wait()
    for copy in copies:
        copy.wait()


def vmem():
    return pl.BlockSpec(memory_space=pltpu.VMEM)


def first_exchange(block, small, weight, members):
    sems = pltpu.SemaphoreType.DMA((members,))
    return pl.pallas_call(
        lambda *refs: first_kernel(members, *refs),
        out_shape=[
            jax.ShapeDtypeStruct((members,) + block.shape, block.dtype),
            jax.ShapeDtypeStruct((members,) + small.shape, small.dtype),
            jax.ShapeDtypeStruct(weight.shape, weight.dtype),
        ],
        in_specs=[vmem()] * 3,
        out_specs=[vmem()] * 3,
        scratch_shapes=[pltpu.SemaphoreType.DMA] + [sems] * 8 + [pltpu.SemaphoreType.DMA((2,))],
        compiler_params=pltpu.CompilerParams(
            collective_id=0, has_side_effects=True, vmem_limit_bytes=24 * 2**20
        ),
        cost_estimate=pl.CostEstimate(flops=0, bytes_accessed=60_000_000, transcendentals=0),
    )(block, small, weight)


def sum_kernel(members, backward, gathers, *refs):
    refs = list(refs)
    left_ref, right_ref, stream_ref, gain_ref = refs[:4]
    refs = refs[4:]
    if backward:
        grad_ref = refs.pop(0)
    result_ref = refs.pop(0)
    if backward:
        gain_out_ref = refs.pop(0)
    if gathers:
        out_ref = refs.pop(0)
    give_ref, pair_ref, ready_ref, land_ref, total_ref, low_ref = refs[:6]
    pair_send, pair_recv, send_sem, recv_sem = refs[6:10]
    me = lax.axis_index("group")
    chips = members // 2
    chip, core = lax.div(me, 2), lax.rem(me, 2)
    sibling = chip * 2 + 1 - core
    barrier = greet(chips, chip, core, sibling)
    pairs = []
    for step in range(chips):
        place = lax.rem(chip + step + 1, chips)
        give_ref[step] = dot(left_ref[place * 2 + 1 - core], right_ref[...]).astype(low)
        if step == 0:
            pl.semaphore_wait(barrier, chips)
        copy = pltpu.make_async_remote_copy(
            src_ref=give_ref.at[step],
            dst_ref=pair_ref.at[step],
            send_sem=pair_send.at[step],
            recv_sem=pair_recv.at[step],
            device_id={"group": sibling},
        )
        copy.start()
        pairs.append(copy)
    sends = []
    for step in range(chips):
        place = lax.rem(chip + step + 1, chips)
        part = dot(left_ref[place * 2 + core], right_ref[...])
        pairs[step].wait_recv()
        part = part + pair_ref[step].astype(jnp.float32)
        if step == chips - 1:
            total_ref[...] = part
            break
        ready_ref[step] = part.astype(low)
        copy = pltpu.make_async_remote_copy(
            src_ref=ready_ref.at[step],
            dst_ref=land_ref.at[step],
            send_sem=send_sem.at[step],
            recv_sem=recv_sem.at[step],
            device_id={"group": place * 2 + core},
        )
        copy.start()
        sends.append(copy)
    for step in range(chips - 1):
        sends[step].wait_recv()
        total_ref[...] += land_ref[step].astype(jnp.float32)
    total = total_ref[...]
    if backward:
        inverse, unit = norm_forward(stream_ref[...])
        gain_out_ref[...] = jnp.sum(total * unit, axis=0, keepdims=True)
        result = grad_ref[...] + norm_back(total * gain_ref[...], unit, inverse)
        result_ref[...] = result
        low_ref[...] = result.astype(low)
    else:
        result = stream_ref[...] + total
        result_ref[...] = result
        if gathers:
            unit = norm_forward(result)[1]
            low_ref[...] = (unit * gain_ref[...]).astype(low)
    if gathers:
        spread(chips, me, low_ref, out_ref, *refs[10:])
    for copy in pairs + sends:
        copy.wait_send()


def block_sum(name, left, right, stream, gain, members, grad=None, gathers=True):
    rows, width = stream.shape
    chips = members // 2
    backward = grad is not None
    outs = [jax.ShapeDtypeStruct((rows, width), jnp.float32)]
    if backward:
        outs.append(jax.ShapeDtypeStruct((1, width), jnp.float32))
    if gathers:
        outs.append(jax.ShapeDtypeStruct((members, rows, width), low))
    operands = [left.reshape(members, rows, left.shape[1]), right, stream, gain[None]]
    if backward:
        operands.append(grad)
    sems = pltpu.SemaphoreType.DMA((chips,))
    scratch = [pltpu.VMEM((chips, rows, width), low) for _ in range(4)]
    scratch += [pltpu.VMEM((rows, width), jnp.float32), pltpu.VMEM((rows, width), low)]
    scratch += [sems] * 4
    if gathers:
        scratch += [pltpu.SemaphoreType.DMA] + [sems] * 4
    result = pl.pallas_call(
        lambda *refs: sum_kernel(members, backward, gathers, *refs),
        out_shape=outs,
        in_specs=[vmem()] * len(operands),
        out_specs=[vmem()] * len(outs),
        scratch_shapes=scratch,
        compiler_params=pltpu.CompilerParams(
            collective_id=name, has_side_effects=True, vmem_limit_bytes=32 * 2**20
        ),
        cost_estimate=pl.CostEstimate(flops=0, bytes_accessed=COST, transcendentals=0),
    )(*operands)
    result = list(result)
    if gathers:
        result[-1] = result[-1].reshape(members * rows, width)
    return result


def swap(blocks):
    return lax.all_to_all(blocks, "group", split_axis=0, concat_axis=0, tiled=True)


def rope_tables(token_positions):
    half_dim = HEAD_DIM // 2
    frequency = rope_base ** (-2.0 * jnp.arange(half_dim, dtype=jnp.float32) / HEAD_DIM)
    angles = token_positions.astype(jnp.float32)[:, None] * frequency[None, :]
    return (jnp.cos(angles)[:, None, :], jnp.sin(angles)[:, None, :])


def rotate(vectors, cosine, sine_table):
    half_dim = HEAD_DIM // 2
    leading, trailing = (vectors[..., :half_dim], vectors[..., half_dim:])
    return jnp.concatenate(
        [leading * cosine - trailing * sine_table, trailing * cosine + leading * sine_table],
        axis=-1,
    )


def norm_forward(stream):
    inverse = lax.rsqrt(jnp.mean(stream * stream, axis=-1, keepdims=True) + epsilon)
    return (inverse, stream * inverse)


def norm_back(grad_unit, unit_value, inverse):
    return inverse * (
        grad_unit - unit_value * jnp.mean(grad_unit * unit_value, axis=-1, keepdims=True)
    )


def pad_columns(matrix, width):
    return jnp.pad(matrix, ((0, 0), (0, width - matrix.shape[1])))


def widen(matrix):
    rows = matrix.shape[0]
    wide = matrix.reshape(rows, KV_HEADS, 1, HEAD_DIM)
    wide = jnp.broadcast_to(wide, (rows, KV_HEADS, SHARE, HEAD_DIM))
    return wide.reshape(rows, HEADS * HEAD_DIM)


def by_member(matrix, members):
    rows, width = matrix.shape
    return matrix.reshape(rows, members, width // members).transpose(1, 0, 2)


def by_row(blocks):
    members, rows, width = blocks.shape
    return blocks.transpose(1, 0, 2).reshape(rows, members * width)


def on_device(
    tokens,
    positions,
    gain_attn,
    w_query,
    w_key,
    w_value,
    w_out,
    gain_ffn,
    w_gate,
    w_up,
    w_down,
    cotangent,
):
    row_count = tokens.shape[1]
    members = lax.axis_size("group")
    owner = lax.axis_index("group")
    length = row_count * members
    own_rows = w_query.shape[1]
    width = own_rows * members
    local_heads = -(-HEADS // members)
    span = local_heads * HEAD_DIM
    padded = span * members
    part_ff = w_gate.shape[2] // members

    def attn_blocks(layer):
        return jnp.concatenate(
            [
                by_member(pad_columns(w_query[layer], padded), members),
                by_member(pad_columns(widen(w_key[layer]), padded), members),
                by_member(pad_columns(widen(w_value[layer]), padded), members),
            ],
            axis=2,
        )

    def ffn_blocks(layer):
        return jnp.concatenate(
            [by_member(w_gate[layer], members), by_member(w_up[layer], members)], axis=2
        )

    lane = 128 * -(-max(row_count, own_rows) // 128)
    small = jnp.concatenate(
        [
            pad_columns(positions.astype(jnp.float32), lane),
            pad_columns(gain_attn.astype(jnp.float32), lane),
            pad_columns(gain_ffn.astype(jnp.float32), lane),
        ],
        axis=0,
    )
    small = jnp.pad(small, ((0, 8 - small.shape[0]), (0, 0)))
    token_blocks, few, first_weight = first_exchange(tokens[0], small, attn_blocks(0), members)
    all_positions = few[:, 0, :row_count].reshape(length).astype(jnp.int32)
    gains = few[:, 1 : 1 + 2 * LAYERS, :own_rows].transpose(1, 0, 2).reshape(2 * LAYERS, width)
    out_low = lax.all_gather(cotangent[0], "group", axis=0, tiled=True)

    weights = []
    for layer in range(LAYERS):
        attn_weight = first_weight if layer == 0 else swap(attn_blocks(layer))
        ffn_weight = swap(ffn_blocks(layer)).reshape(width, 2 * part_ff)
        weights.append([attn_weight.reshape(width, 3 * span), ffn_weight])
    next_out = lax.ppermute(
        w_out, "group", [(member, member - 1) for member in range(1, members)]
    )
    slab = jnp.concatenate(
        [w_out, next_out, jnp.zeros((LAYERS, span - own_rows, width), w_out.dtype)], axis=1
    )
    out_all = lax.dynamic_slice_in_dim(slab, owner * (span - own_rows), span, 1)

    token_index = jnp.arange(length, dtype=jnp.int32)
    allowed = (token_index[None, :] <= token_index[:, None]) & (
        token_index[None, :] >= (token_index - all_positions)[:, None]
    )
    cosine, sine_table = rope_tables(all_positions)

    def heads_of(matrix):
        return matrix.reshape(length, local_heads, HEAD_DIM)

    stream = tokens[0].astype(jnp.float32)
    unit_all = norm_forward(token_blocks.reshape(length, width).astype(jnp.float32))[1]
    normed_attn = (unit_all * gains[0]).astype(low)
    saved_all = []
    outputs = []
    for layer in range(LAYERS):
        attn_weight, ffn_weight = weights[layer]
        product = dot(normed_attn, attn_weight)
        queries = rotate(heads_of(product[:, :span]), cosine, sine_table).astype(low)
        keys = rotate(heads_of(product[:, span : 2 * span]), cosine, sine_table).astype(low)
        values = heads_of(product[:, 2 * span :]).astype(low)
        scores = (
            jnp.einsum("thd,shd->hts", queries, keys, preferred_element_type=jnp.float32) * 0.125
        )
        scores = jnp.where(allowed[None], scores, -1e30)
        exponent = jnp.exp(scores - jnp.max(scores, axis=-1, keepdims=True))
        probs = (exponent / jnp.sum(exponent, axis=-1, keepdims=True)).astype(low)
        mixed = jnp.einsum("hts,shd->thd", probs, values, preferred_element_type=jnp.float32)
        mixed = mixed.reshape(length, span).astype(low)
        after, normed_ffn = block_sum(
            1, mixed, out_all[layer], stream, gains[LAYERS + layer], members
        )
        both = dot(normed_ffn, ffn_weight)
        gate, up = both[:, :part_ff], both[:, part_ff:]
        hidden = (jax.nn.silu(gate) * up).astype(low)
        saved_all.append(
            (stream, normed_attn, queries, keys, values, probs, mixed, after, normed_ffn, gate, up, hidden)
        )
        if layer + 1 < LAYERS:
            stream, normed_attn = block_sum(
                2, hidden, w_down[layer], after, gains[layer + 1], members
            )
        else:
            stream = block_sum(
                3, hidden, w_down[layer], after, gains[layer], members, gathers=False
            )[0]
        outputs.append(stream)

    def narrow(blocks):
        wide = by_row(blocks)[:, : HEADS * HEAD_DIM].astype(jnp.float32)
        wide = wide.reshape(own_rows, KV_HEADS, SHARE, HEAD_DIM)
        return wide.sum(axis=2).reshape(own_rows, KV_HEADS * HEAD_DIM).astype(low)

    grad_result = cotangent[0].astype(jnp.float32)
    gain_sums = [None] * (2 * LAYERS)
    attn_shares = ()
    groups = []

    def replica_sum(shares):
        if groups:
            shares, groups[-1] = lax.optimization_barrier((shares, groups[-1]))
        groups.append(lax.psum(shares, "replica"))

    for layer in reversed(range(LAYERS)):
        attn_weight, ffn_weight = weights[layer]
        (
            stream, normed_attn, queries, keys, values, probs, mixed, after, normed_ffn, gate, up, hidden
        ) = saved_all[layer]
        grad_hidden = against(out_low, w_down[layer])
        sigmoid = jax.nn.sigmoid(gate)
        grad_up = (grad_hidden * gate * sigmoid).astype(low)
        grad_gate = (grad_hidden * up * sigmoid * (1.0 + gate * (1.0 - sigmoid))).astype(low)
        grad_both = jnp.concatenate([grad_gate, grad_up], axis=1)
        if groups:
            grad_both, groups[-1] = lax.optimization_barrier((grad_both, groups[-1]))
        grad_after, gain_sums[LAYERS + layer], after_low = block_sum(
            4, grad_both, ffn_weight.T, after, gains[LAYERS + layer], members, grad=grad_result
        )
        grad_down = over_rows(hidden, out_low).astype(low)
        grad_ffn_weight = swap(
            over_rows(normed_ffn, grad_both).astype(low).reshape(members, own_rows, 2 * part_ff)
        )
        shares = (
            by_row(grad_ffn_weight[:, :, :part_ff]),
            by_row(grad_ffn_weight[:, :, part_ff:]),
            grad_down,
        ) + attn_shares
        after_low, shares = lax.optimization_barrier((after_low, shares))
        replica_sum(shares)
        grad_mixed = against(after_low, out_all[layer]).astype(low)
        grad_out = over_rows(mixed, after_low).astype(low)
        delta = jnp.sum(
            heads_of(grad_mixed.astype(jnp.float32) * mixed.astype(jnp.float32)), axis=-1
        ).T[:, :, None]
        grad_heads = heads_of(grad_mixed)
        grad_probs = jnp.einsum(
            "thd,shd->hts", grad_heads, values, preferred_element_type=jnp.float32
        )
        grad_values = jnp.einsum(
            "hts,thd->shd", probs, grad_heads, preferred_element_type=jnp.float32
        )
        grad_scores = (probs.astype(jnp.float32) * (grad_probs - delta)).astype(low)
        grad_queries = 0.125 * jnp.einsum(
            "hts,shd->thd", grad_scores, keys, preferred_element_type=jnp.float32
        )
        grad_keys = 0.125 * jnp.einsum(
            "hts,thd->shd", grad_scores, queries, preferred_element_type=jnp.float32
        )
        back = jnp.concatenate(
            [
                rotate(grad_queries, cosine, -sine_table).reshape(length, span),
                rotate(grad_keys, cosine, -sine_table).reshape(length, span),
                grad_values.reshape(length, span),
            ],
            axis=1,
        ).astype(low)
        grad_attn_weight = swap(
            over_rows(normed_attn, back).astype(low).reshape(members, own_rows, 3 * span)
        )
        before = lax.ppermute(
            grad_out, "group", [(member, member + 1) for member in range(members - 1)]
        )
        own_out = lax.dynamic_slice_in_dim(
            jnp.concatenate([before, grad_out], axis=0),
            span - owner * (span - own_rows),
            own_rows,
            0,
        )
        attn_shares = (
            by_row(grad_attn_weight[:, :, :span])[:, : HEADS * HEAD_DIM],
            narrow(grad_attn_weight[:, :, span : 2 * span]),
            narrow(grad_attn_weight[:, :, 2 * span :]),
            own_out,
        )
        if layer + 1 == LAYERS:
            back, outputs[-1] = lax.optimization_barrier((back, outputs[-1]))
        if layer > 0:
            grad_result, gain_sums[layer], out_low = block_sum(
                5, back, attn_weight.T, stream, gains[layer], members, grad=grad_after
            )
            out_low, attn_shares = lax.optimization_barrier((out_low, attn_shares))
        else:
            attn_shares, back = lax.optimization_barrier((attn_shares, back))
            grad_result, gain_sums[layer] = block_sum(
                6, back, attn_weight.T, stream, gains[layer], members, grad=grad_after, gathers=False
            )
            grad_result, attn_shares = lax.optimization_barrier((grad_result, attn_shares))
            replica_sum(attn_shares)
    owned = [None] * LAYERS
    for layer in range(LAYERS):
        place = LAYERS - 1 - layer
        owned[layer] = groups[place + 1][-4:] + groups[place][:3]
    if LAYERS > 1:
        owned[0] = groups[LAYERS][:4] + groups[LAYERS - 1][:3]

    gain_total = lax.psum(jnp.concatenate(gain_sums, axis=0), ("group", "replica"))
    gain_total = lax.dynamic_slice_in_dim(gain_total, owner * own_rows, own_rows, 1)
    stacked = [
        jnp.stack([owned[layer][place] for layer in range(LAYERS)]).astype(jnp.float32)
        for place in range(7)
    ]
    return (
        jnp.stack(outputs)[None],
        grad_result[None],
        gain_total[:LAYERS],
        stacked[0],
        stacked[1],
        stacked[2],
        stacked[3],
        gain_total[LAYERS:],
        stacked[4],
        stacked[5],
        stacked[6],
    )


def solution(mesh):
    rows = P(None, "group", None)
    in_specs = (
        P("replica", "group", None),
        P("replica", "group"),
        P(None, "group"),
        rows,
        rows,
        rows,
        rows,
        P(None, "group"),
        rows,
        rows,
        rows,
        P("replica", "group", None),
    )
    out_specs = (
        P("replica", None, "group", None),
        P("replica", "group", None),
        P(None, "group"),
        rows,
        rows,
        rows,
        rows,
        P(None, "group"),
        rows,
        rows,
        rows,
    )
    return jax.shard_map(
        on_device, mesh=mesh, in_specs=in_specs, out_specs=out_specs, check_vma=False
    )
```
